256 devices in a mesh: inner: 32 (over z_hi, x, y), outer: 8 (over z_lo, core).
Axes of the slice: x: 4, y: 4, z: 8 (z_hi: 2, z_lo: 4; z = z_hi * 4 + z_lo), core: 2. Of those that a mesh axis runs over, the one named last changes fastest.
Arguments:
- queries: bfloat16 [131072, 8, 128], P(('inner', 'outer')), may hold values from -6 to 6
- key_tokens: bfloat16 [131072, 128], P(('inner', 'outer')), may hold values from -6 to 6
- value_tokens: bfloat16 [131072, 128], P(('inner', 'outer')), may hold values from -6 to 6
- out_grad: bfloat16 [131072, 8, 128], P(('inner', 'outer')), may hold values from -4 to 4
- forward_out: bfloat16 [131072, 8, 128], P(('inner', 'outer')), may hold values from -4 to 4
- log_norm: float32 [131072, 8], P(('inner', 'outer')), may hold values from 2 to 5
- block_list: int32 [1024, 8], P(('inner', 'outer')), may hold values from 0 to 1023, as said below
- block_live: int32 [1024], P(('inner', 'outer')), may hold values from 1 to 8
Outputs:
- query_grad: bfloat16 [131072, 8, 128], P(('inner', 'outer'))
- key_grad: bfloat16 [131072, 128], P(('inner', 'outer'))
- value_grad: bfloat16 [131072, 128], P(('inner', 'outer'))
The draws below stay inside these ranges and needn't reach their ends.
Inputs may be any that keep to these rules, and one draw needn't show every extreme that they name: `block_list`: for query block b the first block_live[b] entries are distinct key block numbers k <= b, always including b itself, with k lying in the tokens of the device that holds b or of the 4 devices before it along inner+outer; the remaining entries equal b. Some query block uses all 8 entries.
All inputs are finite; a program needn't handle non-finite values.
Results may differ from the reference program's by a relative error of at most 0.0056.
Values may be sent and summed in bfloat16 or wider, within the bound.
No kernel may reach another device: no remote copies, remote signals or barrier semaphores. Data moves between devices by JAX's collectives and lax.ppermute only.
A program may use at most 64 MiB of HBM per device.

```python
import jax
import jax.numpy as jnp
from jax import lax

HEADS = 8
HD = 128
BLOCK = 128
NNZ = 8
REACH = 4
TOK_DEV = 512
TOKENS = 131072
QBLOCKS = 1024


def mask_tables(key):
    per_device = TOK_DEV // BLOCK
    width = max((REACH + 1) * per_device, NNZ)
    query_block = jnp.arange(QBLOCKS, dtype=jnp.int32)
    offsets = jnp.arange(width, dtype=jnp.int32)
    avail = jnp.minimum(query_block + 1, query_block % per_device + REACH * per_device + 1)
    first, second, third = jax.random.split(key, 3)
    scores = jax.random.randint(first, (QBLOCKS, width), 0, 1 << 20, dtype=jnp.int32) * width + offsets[None, :]
    scores = jnp.where(offsets[None, :] == 0, jnp.int32((1 << 20) * width + width), scores)
    scores = jnp.where(offsets[None, :] >= avail[:, None], -1 - offsets[None, :], scores)
    unused, chosen = lax.top_k(scores, NNZ)
    spread = jax.random.randint(second, (QBLOCKS,), 0, NNZ + 1, dtype=jnp.int32)
    live_count = 1 + spread * spread // NNZ
    live_count = jnp.minimum(jnp.minimum(live_count, NNZ), avail)
    forced = jax.random.randint(third, (), NNZ - 1, QBLOCKS, dtype=jnp.int32)
    live_count = jnp.where(query_block == forced, NNZ, live_count).astype(jnp.int32)
    slot_order = jnp.arange(NNZ, dtype=jnp.int32)
    in_use = slot_order[None, :] < live_count[:, None]
    listed = jnp.where(in_use, query_block[:, None] - chosen.astype(jnp.int32), query_block[:, None])
    return (listed.astype(jnp.int32), live_count)


def draw_block_list(key, part):
    listed, live_count = mask_tables(key)
    return listed


def draw_block_live(key, part):
    listed, live_count = mask_tables(key)
    return live_count


def level_of(own_key, shape, cuts, low, largest):
    level = 1.0
    for dim, parts in cuts:
        steps = jax.random.uniform(jax.random.fold_in(jax.random.fold_in(own_key, 6), dim), (parts,), jnp.float32, low / len(cuts), largest / len(cuts))
        level = level * jnp.repeat(jnp.exp(steps), shape[dim] // parts).reshape((-1,) + (1,) * (len(shape) - 1 - dim))
    return level


def scatter_about(key, dims, scale, most, cuts=(), kind=jnp.bfloat16):
    values = scale * jax.random.normal(key, dims, jnp.float32)
    if cuts:
        values = values * level_of(key, dims, cuts, -0.22, 0.18)
    return jnp.clip(values, -most, most).astype(kind)


def setup_inputs(seed: int = 0) -> dict:
    keys = jax.random.split(jax.random.key(seed), 9)
    queries = scatter_about(keys[0], (TOKENS, HEADS, HD), 1.0, 6.0, ((0, 256),))
    key_tokens = scatter_about(keys[1], (TOKENS, HD), 1.0, 6.0, ((0, 256),))
    value_tokens = scatter_about(keys[2], (TOKENS, HD), 1.0, 6.0, ((0, 256),))
    out_grad = scatter_about(keys[3], (TOKENS, HEADS, HD), 0.3, 4.0, ((0, 256),))
    forward_out = scatter_about(keys[4], (TOKENS, HEADS, HD), 0.3, 4.0, ((0, 256),))
    log_norm = jnp.clip(2.0 + 3.0 * jax.random.uniform(keys[5], (TOKENS, HEADS), jnp.float32) ** level_of(keys[5], (TOKENS, HEADS), ((0, 256),), -0.2, 0.2), 2.0, 5.0)
    block_list = draw_block_list(jax.random.fold_in(keys[8], 71), 0)
    block_live = draw_block_live(jax.random.fold_in(keys[8], 71), 0)
    return {"queries": queries, "key_tokens": key_tokens, "value_tokens": value_tokens, "out_grad": out_grad, "forward_out": forward_out, "log_norm": log_norm, "block_list": block_list, "block_live": block_live}


def reference(queries, key_tokens, value_tokens, out_grad, forward_out, log_norm, block_list, block_live):
    row_count = BLOCK * HEADS
    score_scale = HD ** -0.5
    per_dev = TOK_DEV // BLOCK
    dev_count = QBLOCKS // per_dev
    span = (REACH + 1) * per_dev
    query_rows = queries.reshape(dev_count, per_dev, row_count, HD)
    grad_rows = out_grad.reshape(dev_count, per_dev, row_count, HD)
    norm_rows = log_norm.reshape(dev_count, per_dev, row_count)
    delta = jnp.sum(out_grad.astype(jnp.float32) * forward_out.astype(jnp.float32), axis=2)
    delta_rows = delta.reshape(dev_count, per_dev, row_count)
    list_rows = block_list.reshape(dev_count, per_dev, NNZ)
    live_rows = block_live.reshape(dev_count, per_dev)
    key_blocks = key_tokens.reshape(QBLOCKS, BLOCK, HD)
    value_blocks = value_tokens.reshape(QBLOCKS, BLOCK, HD)
    slot_order = jnp.arange(NNZ, dtype=jnp.int32)
    inside = jnp.arange(BLOCK, dtype=jnp.int32)

    def device_step(total, dev_inputs):
        device, dq, dg, dn, dd, dl, dlive = dev_inputs
        window_base = (device - REACH) * per_dev

        def block_step(local_acc, inputs):
            local_index, qrows, grows, nrows, drows, listed, live_count = inputs
            block_index = device * per_dev + local_index
            keys_picked = key_blocks[listed].astype(jnp.float32)
            values_picked = value_blocks[listed].astype(jnp.float32)
            query_float = qrows.astype(jnp.float32)
            grad_float = grows.astype(jnp.float32)
            scores = jnp.einsum('rd,jcd->rjc', query_float, keys_picked) * score_scale
            query_pos = block_index * BLOCK + jnp.arange(row_count, dtype=jnp.int32) // HEADS
            key_pos = listed[:, None] * BLOCK + inside[None, :]
            allowed = (key_pos[None, :, :] <= query_pos[:, None, None]) & (slot_order < live_count)[None, :, None]
            weights = jnp.where(allowed, jnp.exp(scores - nrows[:, None, None]), jnp.float32(0.0))
            weights_low = weights.astype(jnp.bfloat16).astype(jnp.float32)
            weight_grad = jnp.einsum('rd,jcd->rjc', grad_float, values_picked)
            score_grad = (weights * (weight_grad - drows[:, None, None])).astype(jnp.bfloat16).astype(jnp.float32)
            query_part = jnp.einsum('rjc,jcd->rd', score_grad, keys_picked) * score_scale
            key_part = jnp.einsum('rjc,rd->jcd', score_grad, query_float) * score_scale
            value_part = jnp.einsum('rjc,rd->jcd', weights_low, grad_float)
            slot_index = (listed - window_base).astype(jnp.int32)
            local_acc = local_acc.at[slot_index].add(jnp.concatenate([key_part, value_part], axis=2))
            return local_acc, query_part.astype(jnp.bfloat16)

        local_start = jnp.zeros((span, BLOCK, 2 * HD), jnp.float32)
        inputs = (jnp.arange(per_dev, dtype=jnp.int32), dq, dg, dn, dd, dl, dlive)
        local_acc, query_blocks = lax.scan(block_step, local_start, inputs)
        remote = lax.optimization_barrier(local_acc[:REACH * per_dev].astype(jnp.bfloat16)).astype(jnp.float32)
        combined = jnp.concatenate([remote, local_acc[REACH * per_dev:]], axis=0)
        start = (device * per_dev).astype(jnp.int32)
        zero = jnp.zeros((), jnp.int32)
        current = lax.dynamic_slice(total, (start, zero, zero), (span, BLOCK, 2 * HD))
        total = lax.dynamic_update_slice(total, current + combined, (start, zero, zero))
        return total, query_blocks

    total_start = jnp.zeros((REACH * per_dev + QBLOCKS, BLOCK, 2 * HD), jnp.float32)
    dev_inputs = (jnp.arange(dev_count, dtype=jnp.int32), query_rows, grad_rows, norm_rows, delta_rows, list_rows, live_rows)
    total, query_blocks = lax.scan(device_step, total_start, dev_inputs)
    summed = total[REACH * per_dev:].reshape(TOKENS, 2 * HD)
    query_grad = query_blocks.reshape(TOKENS, HEADS, HD)
    key_grad = summed[:, :HD].astype(jnp.bfloat16)
    value_grad = summed[:, HD:].astype(jnp.bfloat16)
    return (query_grad, key_grad, value_grad)
```

```python
import functools

import jax
import jax.numpy as jnp
from jax import lax
from jax.experimental import pallas as pl
from jax.experimental.pallas import tpu as pltpu
from jax.sharding import PartitionSpec as P

BLOCK = 128
AXES = ("inner", "outer")
LOG2E = 1.4426950408889634
NT = (((1,), (1,)), ((), ()))
TN = (((0,), (0,)), ((), ()))
F32 = jnp.float32
BF16 = jnp.bfloat16


def ring_shift(block, distance):
    count = lax.axis_size(AXES)
    route = [(i, (i + distance) % count) for i in range(count)]
    return lax.ppermute(block, AXES, route)


def pair_swap(block):
    count = lax.axis_size(AXES)
    return lax.ppermute(block, AXES, [(i, i ^ 1) for i in range(count)])


def tile_terms(keys, values, qrows, grows, norm, delta, scale, mask=None):
    score = lax.dot_general(keys, qrows, NT, preferred_element_type=F32)
    dweight = lax.dot_general(values, grows, NT, preferred_element_type=F32)
    weight = jnp.exp2(score * (scale * LOG2E) - norm)
    if mask is not None:
        weight = jnp.where(mask, weight, 0.0)
    score_grad = (weight * (dweight - delta)).astype(BF16)
    value_part = jnp.dot(weight.astype(BF16), grows, preferred_element_type=F32)
    key_part = jnp.dot(score_grad, qrows, preferred_element_type=F32)
    query_part = lax.dot_general(keys, score_grad, TN, preferred_element_type=F32)
    return query_part, key_part, value_part


def listed_slots(position, list_ref, live_ref, low, high, visit):
    step = pl.program_id(0)
    local_blocks = pl.num_programs(0)
    own = position * local_blocks + step

    def one(slot, carry):
        block = list_ref[step, slot]
        back = position - block // local_blocks

        @pl.when((back >= low) & (back <= high) & (block != own))
        def _():
            visit(back, block % local_blocks)

        return carry

    lax.fori_loop(0, live_ref[step], one, 0)


def own_kernel(
    position_ref, list_ref, live_ref, q_ref, g_ref, o_ref, norm_ref, k_ref, v_ref,
    delta_ref, dq_ref, dk_ref, dv_ref, *, scale,
):
    step = pl.program_id(0)
    rows, head_size = q_ref.shape
    heads = rows // BLOCK

    @pl.when(step == 0)
    def _():
        dk_ref[...] = jnp.zeros_like(dk_ref)
        dv_ref[...] = jnp.zeros_like(dv_ref)

    product = g_ref[...].astype(F32) * o_ref[...].astype(F32)
    high = product.astype(BF16)
    low = (product - high.astype(F32)).astype(BF16)
    ones = jnp.ones((8, head_size), BF16)
    delta = lax.dot_general(ones, high, NT, preferred_element_type=F32)
    delta = delta + lax.dot_general(ones, low, NT, preferred_element_type=F32)
    delta_ref[0] = delta[:1]

    base = pl.multiple_of(step * BLOCK, BLOCK)
    pieces = 4
    width = rows // pieces
    tokens = BLOCK // pieces
    for piece in range(pieces):
        seen = tokens * (piece + 1)
        span = pl.ds(piece * width, width)
        keys = k_ref[pl.ds(base, seen), :]
        values = v_ref[pl.ds(base, seen), :]
        key_pos = lax.broadcasted_iota(jnp.int32, (seen, width), 0)
        row_pos = lax.broadcasted_iota(jnp.int32, (seen, width), 1)
        mask = key_pos <= piece * tokens + row_pos // heads
        dq, dk, dv = tile_terms(
            keys, values, q_ref[span, :], g_ref[span, :], norm_ref[0, :, span],
            delta_ref[0, :, span], scale, mask,
        )
        dq_ref[0, :, span] = dq
        dk_ref[pl.ds(base, seen), :] += dk * scale
        dv_ref[pl.ds(base, seen), :] += dv

    def visit(back, local):
        at = pl.ds(pl.multiple_of(local * BLOCK, BLOCK), BLOCK)
        dq, dk, dv = tile_terms(
            k_ref[at, :], v_ref[at, :], q_ref[...], g_ref[...], norm_ref[0], delta_ref[0], scale
        )
        dq_ref[0] += dq
        dk_ref[at, :] += dk * scale
        dv_ref[at, :] += dv

    listed_slots(position_ref[0], list_ref, live_ref, 0, 0, visit)


def far_kernel(
    position_ref, list_ref, live_ref, q_ref, g_ref, norm_ref, delta_ref, dq_in_ref,
    ka_ref, va_ref, kb_ref, vb_ref,
    dq_ref, dka_ref, dva_ref, dkb_ref, dvb_ref, k_all, v_all, dk_acc, dv_acc, dq_acc,
    *, scale, low, last,
):
    step = pl.program_id(0)
    count = ka_ref.shape[0]

    @pl.when(step == 0)
    def _():
        k_all[pl.ds(0, count), :] = ka_ref[...]
        k_all[pl.ds(count, count), :] = kb_ref[...]
        v_all[pl.ds(0, count), :] = va_ref[...]
        v_all[pl.ds(count, count), :] = vb_ref[...]
        dk_acc[...] = jnp.zeros_like(dk_acc)
        dv_acc[...] = jnp.zeros_like(dv_acc)

    dq_acc[...] = dq_in_ref[0]

    def visit(back, local):
        at = pl.ds(pl.multiple_of((back - low) * count + local * BLOCK, BLOCK), BLOCK)
        dq, dk, dv = tile_terms(
            k_all[at, :], v_all[at, :], q_ref[...], g_ref[...], norm_ref[0], delta_ref[0], scale
        )
        dq_acc[...] += dq
        dk_acc[at, :] += dk
        dv_acc[at, :] += dv

    listed_slots(position_ref[0], list_ref, live_ref, low, low + 1, visit)

    if last:
        dq_ref[...] = (dq_acc[...] * scale).T.astype(dq_ref.dtype)
    else:
        dq_ref[0] = dq_acc[...]

    @pl.when(step == pl.num_programs(0) - 1)
    def _():
        dka_ref[...] = (dk_acc[pl.ds(0, count), :] * scale).astype(BF16)
        dkb_ref[...] = (dk_acc[pl.ds(count, count), :] * scale).astype(BF16)
        dva_ref[...] = dv_acc[pl.ds(0, count), :].astype(BF16)
        dvb_ref[...] = dv_acc[pl.ds(count, count), :].astype(BF16)


def body(
    queries, key_tokens, value_tokens, out_grad, forward_out, log_norm, block_list, block_live
):
    local_tokens, heads, head_size = queries.shape
    local_blocks = local_tokens // BLOCK
    rows = BLOCK * heads
    scale = head_size ** (-0.5)
    position = lax.axis_index(AXES).astype(jnp.int32)
    odd = lax.axis_index("outer") % 2 == 1
    scalars = (position.reshape(1), block_list, block_live)
    q = queries.reshape(local_blocks * rows, head_size)
    g = out_grad.reshape(local_blocks * rows, head_size)
    o = forward_out.reshape(local_blocks * rows, head_size)
    norm = (log_norm * LOG2E).reshape(local_blocks, 1, rows)

    row_spec = pl.BlockSpec((rows, head_size), lambda i, *_: (i, 0))
    line_spec = pl.BlockSpec((1, 1, rows), lambda i, *_: (i, 0, 0))
    dq_spec = pl.BlockSpec((1, head_size, rows), lambda i, *_: (i, 0, 0))
    shard_spec = pl.BlockSpec((local_tokens, head_size), lambda i, *_: (0, 0))
    line_shape = jax.ShapeDtypeStruct((local_blocks, 1, rows), F32)
    dq_shape = jax.ShapeDtypeStruct((local_blocks, head_size, rows), F32)
    part_shape = jax.ShapeDtypeStruct((local_tokens, head_size), BF16)
    wide_shape = jax.ShapeDtypeStruct((local_tokens, head_size), F32)
    params = pltpu.CompilerParams(
        dimension_semantics=("arbitrary",), vmem_limit_bytes=32 * 1024 * 1024
    )

    def cost(slots):
        return pl.CostEstimate(
            flops=slots * 10 * rows * BLOCK * head_size,
            bytes_accessed=4 * 1024 * 1024,
            transcendentals=slots * rows * BLOCK,
        )

    def own_call():
        return pl.pallas_call(
            functools.partial(own_kernel, scale=scale),
            grid_spec=pltpu.PrefetchScalarGridSpec(
                num_scalar_prefetch=3,
                grid=(local_blocks,),
                in_specs=[row_spec, row_spec, row_spec, line_spec, shard_spec, shard_spec],
                out_specs=[line_spec, dq_spec, shard_spec, shard_spec],
            ),
            out_shape=[line_shape, dq_shape, wide_shape, wide_shape],
            compiler_params=params,
            cost_estimate=cost(8),
            name="own_shard",
        )(*scalars, q, g, o, norm, key_tokens, value_tokens)

    def far_call(dq, delta, ka, va, kb, vb, low, last):
        wide = pltpu.VMEM((2 * local_tokens, head_size), F32)
        narrow = pltpu.VMEM((2 * local_tokens, head_size), BF16)
        return pl.pallas_call(
            functools.partial(far_kernel, scale=scale, low=low, last=last),
            grid_spec=pltpu.PrefetchScalarGridSpec(
                num_scalar_prefetch=3,
                grid=(local_blocks,),
                in_specs=[row_spec, row_spec, line_spec, line_spec, dq_spec] + [shard_spec] * 4,
                out_specs=[row_spec if last else dq_spec] + [shard_spec] * 4,
                scratch_shapes=[narrow, narrow, wide, wide, pltpu.VMEM((head_size, rows), F32)],
            ),
            out_shape=[
                jax.ShapeDtypeStruct(q.shape, BF16) if last else dq_shape
            ] + [part_shape] * 4,
            compiler_params=params,
            cost_estimate=cost(6),
            name="far_shards" if last else "near_shards",
        )(*scalars, q, g, norm, delta, dq, ka, va, kb, vb)

    k2 = ring_shift(key_tokens, 2)
    v2 = ring_shift(value_tokens, 2)
    k4 = ring_shift(k2, 2)
    v4 = ring_shift(v2, 2)
    delta, dq, dk0, dv0 = own_call()
    k1 = pair_swap(jnp.where(odd, k2, key_tokens))
    v1 = pair_swap(jnp.where(odd, v2, value_tokens))
    dq, dk1, dv1, dk2, dv2 = far_call(dq, delta, k1, v1, k2, v2, 1, False)
    k3 = pair_swap(jnp.where(odd, k4, k2))
    v3 = pair_swap(jnp.where(odd, v4, v2))
    dq, dk3, dv3, dk4, dv4 = far_call(dq, delta, k3, v3, k4, v4, 3, True)

    def give_back(own, part1, part2, part3, part4):
        zero = jnp.zeros((), F32)
        other3 = pair_swap(part3).astype(F32)
        other1 = pair_swap(part1).astype(F32)
        far = (part4.astype(F32) + jnp.where(odd, other3, zero)).astype(BF16)
        relayed = ring_shift(far, -2).astype(F32)
        near = part2.astype(F32) + jnp.where(odd, other1, other3) + relayed
        arrived = ring_shift(near.astype(BF16), -2).astype(F32)
        return (own + jnp.where(odd, zero, other1) + arrived).astype(BF16)

    key_grad = give_back(dk0, dk1, dk2, dk3, dk4)
    value_grad = give_back(dv0, dv1, dv2, dv3, dv4)
    return dq.reshape(queries.shape), key_grad, value_grad


def solution(mesh):
    tokens = P(AXES, None)
    wide = P(AXES, None, None)
    return jax.shard_map(
        body,
        mesh=mesh,
        in_specs=(wide, tokens, tokens, wide, wide, tokens, tokens, P(AXES)),
        out_specs=(wide, tokens, tokens),
        check_vma=False,
    )
```

```python
import functools

import jax
import jax.numpy as jnp
from jax import lax
from jax.experimental import pallas as pl
from jax.experimental.pallas import tpu as pltpu
from jax.sharding import PartitionSpec as P

BLOCK = 128
AXES = ("inner", "outer")
LOG2E = 1.4426950408889634
NT = (((1,), (1,)), ((), ()))
TN = (((0,), (0,)), ((), ()))
F32 = jnp.float32
BF16 = jnp.bfloat16


def ring_shift(block, distance):
    count = lax.axis_size(AXES)
    route = [(i, (i + distance) % count) for i in range(count)]
    return lax.ppermute(block, AXES, route)


def pair_swap(block):
    count = lax.axis_size(AXES)
    return lax.ppermute(block, AXES, [(i, i ^ 1) for i in range(count)])


def tile_terms(keys, values, qrows, grows, norm, delta, scale, mask=None):
    score = lax.dot_general(keys, qrows, NT, preferred_element_type=F32)
    dweight = lax.dot_general(values, grows, NT, preferred_element_type=F32)
    weight = jnp.exp2(score * (scale * LOG2E) - norm)
    if mask is not None:
        weight = jnp.where(mask, weight, 0.0)
    score_grad = (weight * (dweight - delta)).astype(BF16)
    value_part = jnp.dot(weight.astype(BF16), grows, preferred_element_type=F32)
    key_part = jnp.dot(score_grad, qrows, preferred_element_type=F32)
    query_part = lax.dot_general(keys, score_grad, TN, preferred_element_type=F32)
    return query_part, key_part, value_part


def block_rows(index, size):
    return pl.ds(pl.multiple_of(index * size, size), size)


def own_place(position, shard):
    return shard == position, 0


def near_place(position, shard):
    back = (position >> 1) - (shard >> 1)
    other = (position ^ shard) & 1
    return (back == 1) | ((back == 0) & (other == 1)), back + (back & other)


def far_place(position, shard):
    back = (position >> 1) - (shard >> 1)
    return back == 2, (position ^ shard) & 1


def listed_items(position, list_ref, live_ref, items_ref, place_of, shards):
    local_blocks, slots = list_ref.shape
    shift = local_blocks.bit_length() - 1
    count = jnp.int32(0)
    for step in range(local_blocks):

        def one(slot, count, step=step):
            block = list_ref[step, slot]
            keep, place = place_of(position, block >> shift)
            keep = keep & (block != position * local_blocks + step)
            local = place * local_blocks + (block & (local_blocks - 1))
            items_ref[count] = step * (shards * local_blocks) + local
            return count + keep.astype(jnp.int32)

        count = lax.fori_loop(0, live_ref[step], one, count)
    return count


def run_items(count, items_ref, per_step, k_ref, v_ref, q_ref, g_ref, norm_ref, delta_ref,
              dq_ref, dk_ref, dv_ref, scale):
    rows = norm_ref.shape[2]

    def some(start, number):
        pairs = []
        for offset in range(number):
            item = items_ref[start + offset]
            pairs.append((item // per_step, item % per_step))
        terms = []
        for step, place in pairs:
            at, span = block_rows(place, BLOCK), block_rows(step, rows)
            terms.append(
                tile_terms(
                    k_ref[at, :], v_ref[at, :], q_ref[span, :], g_ref[span, :],
                    norm_ref[step], delta_ref[step], scale,
                )
            )
        for (step, place), (dq, dk, dv) in zip(pairs, terms):
            at = block_rows(place, BLOCK)
            dq_ref[step] += dq
            dk_ref[at, :] += dk
            dv_ref[at, :] += dv

    def two(index, carry):
        some(index * 2, 2)
        return carry

    lax.fori_loop(0, count // 2, two, 0)

    @pl.when(count % 2 == 1)
    def _():
        some(count - 1, 1)


def own_kernel(
    position_ref, list_hbm, live_hbm, q_hbm, g_hbm, o_hbm, norm_hbm, k_hbm, v_hbm,
    list_out, live_out, q_ref, g_ref, norm_ref, delta_ref, dq_ref, dk_ref, dv_ref, both_ref,
    o_ref, raw_ref, list_ref, live_ref, items_ref, row_sems, sems, *, scale,
):
    local_blocks = list_ref.shape[0]
    head_size = q_ref.shape[1]
    rows = norm_ref.shape[2]
    heads = rows // BLOCK
    tokens = local_blocks * BLOCK
    k_ref, v_ref = both_ref.at[pl.ds(0, tokens), :], both_ref.at[pl.ds(tokens, tokens), :]
    single = [
        pltpu.make_async_copy(source, target, sems.at[index])
        for index, (source, target) in enumerate(
            (
                (norm_hbm, raw_ref), (k_hbm, k_ref), (v_hbm, v_ref), (list_hbm, list_ref),
                (live_hbm, live_ref), (list_hbm, list_out), (live_hbm, live_out),
            )
        )
    ]
    moves = []
    for step in range(local_blocks):
        span = pl.ds(step * rows, rows)
        moves.append([
            pltpu.make_async_copy(source.at[span, :], target.at[span, :], row_sems.at[index, step])
            for index, (source, target) in enumerate(
                ((g_hbm, g_ref), (o_hbm, o_ref), (q_hbm, q_ref))
            )
        ])
    for copy in moves[0] + single + moves[1] + moves[2] + moves[3]:
        copy.start()
    ones = jnp.ones((8, 2 * head_size), BF16)
    key_pos = lax.broadcasted_iota(jnp.int32, (BLOCK, rows), 0)
    row_pos = lax.broadcasted_iota(jnp.int32, (BLOCK, rows), 1)
    mask = key_pos * heads <= row_pos
    same_token = jnp.where(key_pos == row_pos // heads, 1.0, 0.0).astype(BF16)
    head_pos = lax.broadcasted_iota(jnp.int32, (3 * heads, rows), 0) % heads
    same_head = head_pos == lax.broadcasted_iota(jnp.int32, (3 * heads, rows), 1) % heads
    for copy in single:
        copy.wait()
    for step in range(local_blocks):
        span = pl.ds(step * rows, rows)
        at = pl.ds(step * BLOCK, BLOCK)
        rest = raw_ref[:, at] * LOG2E
        pieces = []
        for _ in range(3):
            pieces.append(rest.astype(BF16).astype(F32))
            rest = rest - pieces[-1]
        pieces = jnp.concatenate(pieces, axis=0).astype(BF16)
        spread = jnp.dot(pieces, same_token, preferred_element_type=F32)
        norm = jnp.sum(jnp.where(same_head, spread, 0.0), axis=0, keepdims=True)
        norm_ref[step] = norm
        for copy in moves[step]:
            copy.wait()
        product = g_ref[span, :].astype(F32) * o_ref[span, :].astype(F32)
        high = product.astype(BF16)
        low = (product - high.astype(F32)).astype(BF16)
        both = jnp.concatenate([high, low], axis=1)
        delta = lax.dot_general(ones, both, NT, preferred_element_type=F32)
        delta_ref[step] = delta[:1]
        dq, dk, dv = tile_terms(
            k_ref[at, :], v_ref[at, :], q_ref[span, :], g_ref[span, :], norm, delta[:1], scale, mask
        )
        dq_ref[step] = dq
        dk_ref[at, :] = dk
        dv_ref[at, :] = dv
    count = listed_items(position_ref[0], list_ref, live_ref, items_ref, own_place, 1)
    run_items(
        count, items_ref, local_blocks, k_ref, v_ref, q_ref, g_ref, norm_ref, delta_ref,
        dq_ref, dk_ref, dv_ref, scale,
    )
    dk_ref[...] = dk_ref[...] * scale


def shards_kernel(position_ref, list_ref, live_ref, q_ref, g_ref, norm_ref, delta_ref, *refs,
                  scale, parts, shards, place_of):
    tokens = list_ref.shape[0] * BLOCK
    inputs = []
    for ref in refs[1 : 1 + parts]:
        inputs += [ref.at[pl.ds(start, tokens), :] for start in range(0, ref.shape[0], tokens)]
    dq_ref = refs[1 + parts]
    outs = refs[2 + parts : -5]
    k_all, v_all, dk_acc, dv_acc, items_ref = refs[-5:]
    count = listed_items(position_ref[0], list_ref, live_ref, items_ref, place_of, shards)
    for index in range(shards):
        span = pl.ds(index * tokens, tokens)
        k_all[span, :] = inputs[2 * index][...]
        v_all[span, :] = inputs[2 * index + 1][...]
    dk_acc[...] = jnp.zeros_like(dk_acc)
    dv_acc[...] = jnp.zeros_like(dv_acc)
    run_items(
        count, items_ref, shards * list_ref.shape[0], k_all, v_all, q_ref, g_ref, norm_ref,
        delta_ref, dq_ref, dk_acc, dv_acc, scale,
    )
    if shards == 3:
        order = ((outs[1], 0, 1), (outs[0], 0, 1), (outs[2], 0, None), (outs[3], None, 0))
        places = (0, 1, 2, 2)
    else:
        order = ((outs[0], 0, 1), (outs[1], 0, 1))
        places = (0, 1)
    for place, (ref, k_half, v_half) in zip(places, order):
        span = pl.ds(place * tokens, tokens)
        if k_half is not None:
            ref[pl.ds(k_half * tokens, tokens), :] = (dk_acc[span, :] * scale).astype(BF16)
        if v_half is not None:
            ref[pl.ds(v_half * tokens, tokens), :] = dv_acc[span, :].astype(BF16)


def finish_kernel(dq_ref, out_ref, *, scale):
    out_ref[...] = (dq_ref[0] * scale).T.astype(out_ref.dtype)


def in_vmem(array):
    return pltpu.with_memory_space_constraint(array, pltpu.VMEM)


def in_hbm(array):
    return pltpu.with_memory_space_constraint(array, pltpu.HBM)


def body(
    queries, key_tokens, value_tokens, out_grad, forward_out, log_norm, block_list, block_live
):
    local_tokens, heads, head_size = queries.shape
    local_blocks, slots = block_list.shape
    rows = BLOCK * heads
    all_rows = (local_blocks * rows, head_size)
    scale = head_size ** (-0.5)
    position = lax.axis_index(AXES).astype(jnp.int32)
    device = position.reshape(1)

    smem = pl.BlockSpec(memory_space=pltpu.SMEM)
    vmem = pl.BlockSpec(memory_space=pltpu.VMEM)
    anywhere = pl.BlockSpec(memory_space=pl.ANY)
    line_shape = pltpu.VMEM((local_blocks, 1, rows), F32)
    rows_shape = pltpu.VMEM(all_rows, BF16)
    dq_shape = pltpu.VMEM((local_blocks, head_size, rows), F32)
    wide_shape = jax.ShapeDtypeStruct((local_tokens, head_size), F32)
    items = pltpu.SMEM((local_blocks * slots + 1,), jnp.int32)
    params = pltpu.CompilerParams(vmem_limit_bytes=24 * 1024 * 1024)

    def stacked(number):
        return jax.ShapeDtypeStruct((number * local_tokens, head_size), BF16)

    def cost(slots):
        return pl.CostEstimate(flops=slots, bytes_accessed=slots, transcendentals=0)

    def own_call():
        outs = pl.pallas_call(
            functools.partial(own_kernel, scale=scale),
            in_specs=[smem] + [anywhere] * 8,
            out_specs=[vmem] * 10,
            out_shape=[pltpu.VMEM(block_list.shape, jnp.int32)]
            + [pltpu.VMEM(block_live.shape, jnp.int32)]
            + [rows_shape] * 2 + [line_shape] * 2 + [dq_shape] + [wide_shape] * 2 + [stacked(2)],
            scratch_shapes=[
                pltpu.VMEM(all_rows, BF16), pltpu.VMEM((heads, local_tokens), F32),
                pltpu.SMEM(block_list.shape, jnp.int32), pltpu.SMEM(block_live.shape, jnp.int32),
                items, pltpu.SemaphoreType.DMA((3, local_blocks)), pltpu.SemaphoreType.DMA((7,)),
            ],
            compiler_params=params,
            cost_estimate=cost(1),
            name="own_shard",
        )(
            device, in_hbm(block_list), in_hbm(block_live),
            in_hbm(queries.reshape(all_rows)), in_hbm(out_grad.reshape(all_rows)),
            in_hbm(forward_out.reshape(all_rows)), in_hbm(log_norm.T),
            in_hbm(key_tokens), in_hbm(value_tokens),
        )
        return [in_vmem(x) for x in outs[:7]] + list(outs[7:])

    def shards_call(dq, parts, shards, place_of, name):
        wide = pltpu.VMEM((shards * local_tokens, head_size), F32)
        narrow = pltpu.VMEM((shards * local_tokens, head_size), BF16)
        return pl.pallas_call(
            functools.partial(
                shards_kernel, scale=scale, parts=len(parts), shards=shards, place_of=place_of
            ),
            in_specs=[smem] * 3 + [vmem] * (5 + len(parts)),
            out_specs=[vmem] * (3 if shards == 2 else 5),
            out_shape=[dq_shape, stacked(2), stacked(2)] + [stacked(1)] * (0 if shards == 2 else 2),
            scratch_shapes=[narrow, narrow, wide, wide, items],
            input_output_aliases={7: 0},
            compiler_params=params,
            cost_estimate=cost(1),
            name=name,
        )(device, listed, live, q, g, norm, delta, in_vmem(dq), *map(in_vmem, parts))

    def finish_call(dq):
        return pl.pallas_call(
            functools.partial(finish_kernel, scale=scale),
            grid=(local_blocks,),
            in_specs=[pl.BlockSpec((1, head_size, rows), lambda i: (i, 0, 0))],
            out_specs=pl.BlockSpec((rows, head_size), lambda i: (i, 0)),
            out_shape=jax.ShapeDtypeStruct(all_rows, BF16),
            compiler_params=params,
            cost_estimate=cost(1),
            name="query_grad",
        )(in_vmem(dq))

    k2, v2 = ring_shift(key_tokens, 2), ring_shift(value_tokens, 2)
    listed, live, q, g, norm, delta, dq, dk0, dv0, kv = own_call()
    k2, v2, kv, dq = lax.optimization_barrier((k2, v2, kv, dq))
    kv2 = jnp.concatenate([k2, v2], axis=0)
    kv4 = ring_shift(kv2, 2)
    dq, near, crossed, crossed_k, crossed_v = shards_call(
        dq, (pair_swap(kv), kv2, pair_swap(kv2)), 3, near_place, "near_shards"
    )
    near = [
        ring_shift(
            (near[i * local_tokens : (i + 1) * local_tokens].astype(F32)
             + pair_swap(part).astype(F32)).astype(BF16),
            -2,
        )
        for i, part in enumerate((crossed_k, crossed_v))
    ]
    kv4, dq = lax.optimization_barrier((kv4, dq))
    dq, far, crossed_far = shards_call(
        dq, (kv4, pair_swap(kv4)), 2, far_place, "far_shards"
    )
    far, crossed_far, near[0], near[1], dq = lax.optimization_barrier(
        (far, crossed_far, near[0], near[1], dq)
    )
    far = (far.astype(F32) + pair_swap(crossed_far).astype(F32)).astype(BF16)
    far = ring_shift(far, -4)
    query_grad = finish_call(dq)
    far, query_grad = lax.optimization_barrier((far, query_grad))
    rest = pair_swap(crossed).astype(F32) + far.astype(F32)
    key_grad = (dk0 + near[0].astype(F32) + rest[:local_tokens]).astype(BF16)
    value_grad = (dv0 + near[1].astype(F32) + rest[local_tokens:]).astype(BF16)
    return query_grad.reshape(queries.shape), key_grad, value_grad


def solution(mesh):
    tokens = P(AXES, None)
    wide = P(AXES, None, None)
    return jax.shard_map(
        body,
        mesh=mesh,
        in_specs=(wide, tokens, tokens, wide, wide, tokens, tokens, P(AXES)),
        out_specs=(wide, tokens, tokens),
        check_vma=False,
    )
```

```python
import functools

import jax
import jax.numpy as jnp
from jax import lax
from jax.experimental import pallas as pl
from jax.experimental.pallas import tpu as pltpu
from jax.sharding import PartitionSpec as P

BLOCK = 128
CODE_BITS = 4
CODES = 1 << CODE_BITS
SPARE = 384
AXES = ("inner", "outer")
LOG2E = 1.4426950408889634
NT = (((1,), (1,)), ((), ()))
TN = (((0,), (0,)), ((), ()))
F32 = jnp.float32
BF16 = jnp.bfloat16


def ring_shift(block, distance):
    count = lax.axis_size(AXES)
    route = [(i, (i + distance) % count) for i in range(count)]
    return lax.ppermute(block, AXES, route)


def pair_swap(block):
    count = lax.axis_size(AXES)
    return lax.ppermute(block, AXES, [(i, i ^ 1) for i in range(count)])


def tile_terms(keys, values, qrows, grows, norm, delta, scale, mask=None):
    score = lax.dot_general(keys, qrows, NT, preferred_element_type=F32)
    dweight = lax.dot_general(values, grows, NT, preferred_element_type=F32)
    weight = jnp.exp2(score * (scale * LOG2E) - norm)
    if mask is not None:
        weight = jnp.where(mask, weight, 0.0)
    score_grad = (weight * (dweight - delta)).astype(BF16)
    value_part = jnp.dot(weight.astype(BF16), grows, preferred_element_type=F32)
    key_part = jnp.dot(score_grad, qrows, preferred_element_type=F32)
    query_part = lax.dot_general(keys, score_grad, TN, preferred_element_type=F32)
    return query_part, key_part, value_part


def block_rows(index, size):
    return pl.ds(pl.multiple_of(index * size, size), size)


def own_place(position, shard):
    return shard == position, 0


def near_place(position, shard):
    back = (position >> 1) - (shard >> 1)
    other = (position ^ shard) & 1
    return (back == 1) | ((back == 0) & (other == 1)), back + (back & other)


def far_place(position, shard):
    back = (position >> 1) - (shard >> 1)
    return back == 2, (position ^ shard) & 1


def listed_items(position, list_ref, live_ref, items_ref, place_of, shards):
    local_blocks, slots = list_ref.shape
    shift = local_blocks.bit_length() - 1
    doubles, singles = jnp.int32(0), jnp.int32(0)
    for step in range(local_blocks):

        def one(slot, carry, step=step):
            doubles, waiting, last = carry
            block = list_ref[step, slot]
            keep, place = place_of(position, block >> shift)
            keep = (keep & (block != position * local_blocks + step)).astype(jnp.int32)
            local = place * local_blocks + (block & (local_blocks - 1))
            code = step * CODES + local
            items_ref[0, doubles] = last * CODES * CODES + code
            doubles = doubles + (keep & waiting)
            return doubles, keep ^ waiting, jnp.where(keep == 1, code, last)

        doubles, waiting, last = lax.fori_loop(
            0, live_ref[step], one, (doubles, jnp.int32(0), jnp.int32(0))
        )
        items_ref[1, singles] = last
        singles = singles + waiting
    return doubles, singles


def run_items(counts, items_ref, k_ref, v_ref, q_ref, g_ref, norm_ref, delta_ref,
              dq_ref, dk_ref, dv_ref, scale):
    rows = norm_ref.shape[2]

    def some(row, start, number):
        entries = []
        for offset in range(number):
            item = items_ref[row, start + offset]
            places = [item & (CODES - 1)]
            if row == 0:
                places.append((item >> (2 * CODE_BITS)) & (CODES - 1))
            entries.append(((item >> CODE_BITS) & (CODES - 1), [block_rows(p, BLOCK) for p in places]))
        terms = []
        for step, spans in entries:
            span = block_rows(step, rows)
            keys = jnp.concatenate([k_ref[at, :] for at in spans], axis=0)
            values = jnp.concatenate([v_ref[at, :] for at in spans], axis=0)
            terms.append(
                tile_terms(
                    keys, values, q_ref[span, :], g_ref[span, :], norm_ref[step], delta_ref[step],
                    scale,
                )
            )
        for (step, spans), (dq, dk, dv) in zip(entries, terms):
            dq_ref[step] += dq
            for index, at in enumerate(spans):
                part = slice(index * BLOCK, (index + 1) * BLOCK)
                dk_ref[at, :] += dk[part]
                dv_ref[at, :] += dv[part]

    for row, count in enumerate(counts):

        def two(index, carry, row=row):
            some(row, index * 2, 2)
            return carry

        lax.fori_loop(0, count // 2, two, 0)

        @pl.when(count % 2 == 1)
        def _(row=row, count=count):
            some(row, count - 1, 1)


def own_kernel(
    position_ref, list_hbm, live_hbm, q_hbm, g_hbm, o_hbm, norm_hbm, k_hbm, v_hbm,
    list_out, live_out, q_ref, g_ref, norm_ref, delta_ref, dq_ref, dk_ref, dv_ref, both_ref,
    o_ref, raw_ref, list_ref, live_ref, items_ref, row_sems, sems, *, scale,
):
    local_blocks = list_ref.shape[0]
    head_size = q_ref.shape[1]
    rows = norm_ref.shape[2]
    heads = rows // BLOCK
    tokens = local_blocks * BLOCK
    k_ref, v_ref = both_ref.at[pl.ds(0, tokens), :], both_ref.at[pl.ds(tokens, tokens), :]
    single = [
        pltpu.make_async_copy(source, target, sems.at[index])
        for index, (source, target) in enumerate(
            (
                (norm_hbm, raw_ref), (k_hbm, k_ref), (v_hbm, v_ref), (list_hbm, list_ref),
                (live_hbm, live_ref), (list_hbm, list_out), (live_hbm, live_out),
            )
        )
    ]
    moves = []
    for step in range(local_blocks):
        span = pl.ds(step * rows, rows)
        moves.append([
            pltpu.make_async_copy(source.at[span, :], target.at[span, :], row_sems.at[index, step])
            for index, (source, target) in enumerate(
                ((g_hbm, g_ref), (o_hbm, o_ref), (q_hbm, q_ref))
            )
        ])
    for copy in moves[0] + single + moves[1] + moves[2] + moves[3]:
        copy.start()
    ones = jnp.ones((8, 2 * head_size), BF16)
    key_pos = lax.broadcasted_iota(jnp.int32, (BLOCK, rows), 0)
    row_pos = lax.broadcasted_iota(jnp.int32, (BLOCK, rows), 1)
    mask = key_pos * heads <= row_pos
    same_token = jnp.where(key_pos == row_pos // heads, 1.0, 0.0).astype(BF16)
    head_pos = lax.broadcasted_iota(jnp.int32, (3 * heads, rows), 0) % heads
    same_head = head_pos == lax.broadcasted_iota(jnp.int32, (3 * heads, rows), 1) % heads
    for copy in single:
        copy.wait()
    for step in range(local_blocks):
        span = pl.ds(step * rows, rows)
        at = pl.ds(step * BLOCK, BLOCK)
        rest = raw_ref[:, at] * LOG2E
        pieces = []
        for _ in range(3):
            pieces.append(rest.astype(BF16).astype(F32))
            rest = rest - pieces[-1]
        pieces = jnp.concatenate(pieces, axis=0).astype(BF16)
        spread = jnp.dot(pieces, same_token, preferred_element_type=F32)
        norm = jnp.sum(jnp.where(same_head, spread, 0.0), axis=0, keepdims=True)
        norm_ref[step] = norm
        for copy in moves[step]:
            copy.wait()
        product = g_ref[span, :].astype(F32) * o_ref[span, :].astype(F32)
        high = product.astype(BF16)
        low = (product - high.astype(F32)).astype(BF16)
        both = jnp.concatenate([high, low], axis=1)
        delta = lax.dot_general(ones, both, NT, preferred_element_type=F32)
        delta_ref[step] = delta[:1]
        dq, dk, dv = tile_terms(
            k_ref[at, :], v_ref[at, :], q_ref[span, :], g_ref[span, :], norm, delta[:1], scale, mask
        )
        dq_ref[step] = dq
        dk_ref[at, :] = dk
        dv_ref[at, :] = dv
    counts = listed_items(position_ref[0], list_ref, live_ref, items_ref, own_place, 1)
    run_items(
        counts, items_ref, k_ref, v_ref, q_ref, g_ref, norm_ref, delta_ref,
        dq_ref, dk_ref, dv_ref, scale,
    )
    dk_ref[...] = dk_ref[...] * scale


def shards_kernel(position_ref, list_ref, live_ref, q_ref, g_ref, norm_ref, delta_ref, *refs,
                  scale, parts, shards, place_of):
    tokens = list_ref.shape[0] * BLOCK
    inputs = []
    for ref in refs[1 : 1 + parts]:
        inputs += [ref.at[pl.ds(start, tokens), :] for start in range(0, ref.shape[0], tokens)]
    dq_ref = refs[1 + parts]
    outs = refs[2 + parts : -5]
    k_all, v_all, dk_acc, dv_acc, items_ref = refs[-5:]
    counts = listed_items(position_ref[0], list_ref, live_ref, items_ref, place_of, shards)
    for index in range(shards):
        span = pl.ds(index * tokens, tokens)
        k_all[span, :] = inputs[2 * index][...]
        v_all[span, :] = inputs[2 * index + 1][...]
    dk_acc[...] = jnp.zeros_like(dk_acc)
    dv_acc[...] = jnp.zeros_like(dv_acc)
    run_items(
        counts, items_ref, k_all, v_all, q_ref, g_ref, norm_ref,
        delta_ref, dq_ref, dk_acc, dv_acc, scale,
    )
    pieces = len(outs) - shards + 1
    size = 2 * tokens // pieces
    for index in range(pieces // 2):
        span = pl.ds((shards - 1) * tokens + index * size, size)
        outs[index][...] = (dk_acc[span, :] * scale).astype(BF16)
        outs[pieces // 2 + index][...] = dv_acc[span, :].astype(BF16)
    for ref, place in zip(outs[pieces:], range(shards - 2, -1, -1)):
        span = pl.ds(place * tokens, tokens)
        ref[pl.ds(0, tokens), :] = (dk_acc[span, :] * scale).astype(BF16)
        ref[pl.ds(tokens, tokens), :] = dv_acc[span, :].astype(BF16)


def add_kernel(straight_ref, *refs, outs):
    crossed, out_refs = refs[:-outs], refs[-outs:]
    size = crossed[0].shape[0]
    whole = len(crossed) * size // outs
    for index, ref in enumerate(crossed):
        span = pl.ds(index * size, size)
        out_span = pl.ds(index * size % whole, size)
        total = straight_ref[span, :].astype(F32) + ref[...].astype(F32)
        out_refs[index * size // whole][out_span, :] = total.astype(BF16)
    if outs == 1:
        span = pl.ds(whole, SPARE)
        out_refs[0][span, :] = jnp.zeros((SPARE, straight_ref.shape[1]), BF16)


def finish_kernel(dq_ref, out_ref, *, scale):
    out_ref[...] = (dq_ref[0] * scale).T.astype(out_ref.dtype)


def in_vmem(array):
    return pltpu.with_memory_space_constraint(array, pltpu.VMEM)


def in_hbm(array):
    return pltpu.with_memory_space_constraint(array, pltpu.HBM)


def body(
    queries, key_tokens, value_tokens, out_grad, forward_out, log_norm, block_list, block_live
):
    local_tokens, heads, head_size = queries.shape
    local_blocks, slots = block_list.shape
    rows = BLOCK * heads
    all_rows = (local_blocks * rows, head_size)
    scale = head_size ** (-0.5)
    position = lax.axis_index(AXES).astype(jnp.int32)
    device = position.reshape(1)

    smem = pl.BlockSpec(memory_space=pltpu.SMEM)
    vmem = pl.BlockSpec(memory_space=pltpu.VMEM)
    anywhere = pl.BlockSpec(memory_space=pl.ANY)
    line_shape = pltpu.VMEM((local_blocks, 1, rows), F32)
    rows_shape = pltpu.VMEM(all_rows, BF16)
    dq_shape = pltpu.VMEM((local_blocks, head_size, rows), F32)
    wide_shape = jax.ShapeDtypeStruct((local_tokens, head_size), F32)
    spare_shape = jax.ShapeDtypeStruct((2 * local_tokens + SPARE, head_size), BF16)
    quarter = jax.ShapeDtypeStruct((local_tokens // 2, head_size), BF16)
    items = pltpu.SMEM((2, local_blocks * slots + 1), jnp.int32)
    params = pltpu.CompilerParams(vmem_limit_bytes=24 * 1024 * 1024)

    def stacked(number):
        return jax.ShapeDtypeStruct((number * local_tokens, head_size), BF16)

    def cost(slots):
        return pl.CostEstimate(flops=slots, bytes_accessed=slots, transcendentals=0)

    def own_call():
        outs = pl.pallas_call(
            functools.partial(own_kernel, scale=scale),
            in_specs=[smem] + [anywhere] * 8,
            out_specs=[vmem] * 10,
            out_shape=[pltpu.VMEM(block_list.shape, jnp.int32)]
            + [pltpu.VMEM(block_live.shape, jnp.int32)]
            + [rows_shape] * 2 + [line_shape] * 2 + [dq_shape] + [wide_shape] * 2 + [stacked(2)],
            scratch_shapes=[
                pltpu.VMEM(all_rows, BF16), pltpu.VMEM((heads, local_tokens), F32),
                pltpu.SMEM(block_list.shape, jnp.int32), pltpu.SMEM(block_live.shape, jnp.int32),
                items, pltpu.SemaphoreType.DMA((3, local_blocks)), pltpu.SemaphoreType.DMA((7,)),
            ],
            compiler_params=params,
            cost_estimate=cost(1),
            name="own_shard",
        )(
            device, in_hbm(block_list), in_hbm(block_live),
            in_hbm(queries.reshape(all_rows)), in_hbm(out_grad.reshape(all_rows)),
            in_hbm(forward_out.reshape(all_rows)), in_hbm(log_norm.T),
            in_hbm(key_tokens), in_hbm(value_tokens),
        )
        return [in_vmem(x) for x in outs[:7]] + list(outs[7:])

    def shards_call(dq, parts, shards, place_of, name):
        wide = pltpu.VMEM((shards * local_tokens, head_size), F32)
        narrow = pltpu.VMEM((shards * local_tokens, head_size), BF16)
        return pl.pallas_call(
            functools.partial(
                shards_kernel, scale=scale, parts=len(parts), shards=shards, place_of=place_of
            ),
            in_specs=[smem] * 3 + [vmem] * (5 + len(parts)),
            out_specs=[vmem] * (shards + (4 if shards == 3 else 2)),
            out_shape=[dq_shape]
            + ([quarter] * 4 if shards == 3 else [stacked(1)] * 2)
            + [stacked(2)] * (shards - 1),
            scratch_shapes=[narrow, narrow, wide, wide, items],
            input_output_aliases={7: 0},
            compiler_params=params,
            cost_estimate=cost(1),
            name=name,
        )(device, listed, live, q, g, norm, delta, in_vmem(dq), *map(in_vmem, parts))

    def add_call(straight, crossed, shapes, name):
        return pl.pallas_call(
            functools.partial(add_kernel, outs=len(shapes)),
            in_specs=[vmem] * (1 + len(crossed)),
            out_specs=[vmem] * len(shapes),
            out_shape=shapes,
            compiler_params=params,
            cost_estimate=cost(1),
            name=name,
        )(*map(in_vmem, (straight, *crossed)))

    def finish_call(dq):
        return pl.pallas_call(
            functools.partial(finish_kernel, scale=scale),
            grid=(local_blocks,),
            in_specs=[pl.BlockSpec((1, head_size, rows), lambda i: (i, 0, 0))],
            out_specs=pl.BlockSpec((rows, head_size), lambda i: (i, 0)),
            out_shape=jax.ShapeDtypeStruct(all_rows, BF16),
            compiler_params=params,
            cost_estimate=cost(1),
            name="query_grad",
        )(in_vmem(dq))

    k2, v2 = ring_shift(key_tokens, 2), ring_shift(value_tokens, 2)
    listed, live, q, g, norm, delta, dq, dk0, dv0, kv = own_call()
    k2, v2, kv, dq = lax.optimization_barrier((k2, v2, kv, dq))
    k4, v4 = ring_shift(k2, 2), ring_shift(v2, 2)
    dq, *crossed, near, other = shards_call(
        dq, (pair_swap(kv), k2, v2, pair_swap(k2), pair_swap(v2)), 3, near_place, "near_shards"
    )
    (near,) = add_call(near, [pair_swap(x) for x in crossed], [spare_shape], "near_sum")
    near = ring_shift(near, -2)
    k4, v4, dq = lax.optimization_barrier((k4, v4, dq))
    dq, *crossed, far = shards_call(
        dq, (k4, v4, pair_swap(k4), pair_swap(v4)), 2, far_place, "far_shards"
    )
    far = add_call(far, [pair_swap(x) for x in crossed], [stacked(1)] * 2, "far_sum")
    far_k, far_v = (ring_shift(part, -4) for part in far)
    near, dq = lax.optimization_barrier((near, dq))
    query_grad = finish_call(dq)
    far_k, far_v, query_grad = lax.optimization_barrier((far_k, far_v, query_grad))
    rest = pair_swap(other).astype(F32) + near[: 2 * local_tokens].astype(F32)
    key_grad = (dk0 + rest[:local_tokens] + far_k.astype(F32)).astype(BF16)
    value_grad = (dv0 + rest[local_tokens:] + far_v.astype(F32)).astype(BF16)
    return query_grad.reshape(queries.shape), key_grad, value_grad


def solution(mesh):
    tokens = P(AXES, None)
    wide = P(AXES, None, None)
    return jax.shard_map(
        body,
        mesh=mesh,
        in_specs=(wide, tokens, tokens, wide, wide, tokens, tokens, P(AXES)),
        out_specs=(wide, tokens, tokens),
        check_vma=False,
    )
```

```python
import functools

import jax
import jax.numpy as jnp
from jax import lax
from jax.experimental import pallas as pl
from jax.experimental.pallas import tpu as pltpu
from jax.sharding import PartitionSpec as P

BLOCK = 128
CODE_BITS = 4
CODES = 1 << CODE_BITS
SPARE = 16
AXES = ("inner", "outer")
LOG2E = 1.4426950408889634
NT = (((1,), (1,)), ((), ()))
TN = (((0,), (0,)), ((), ()))
F32 = jnp.float32
BF16 = jnp.bfloat16


def ring_shift(block, distance):
    count = lax.axis_size(AXES)
    route = [(i, (i + distance) % count) for i in range(count)]
    return lax.ppermute(block, AXES, route)


def pair_swap(block):
    count = lax.axis_size(AXES)
    return lax.ppermute(block, AXES, [(i, i ^ 1) for i in range(count)])


def tile_terms(keys, values, qrows, grows, norm, delta, scale, mask=None):
    score = lax.dot_general(keys, qrows, NT, preferred_element_type=F32)
    dweight = lax.dot_general(values, grows, NT, preferred_element_type=F32)
    weight = jnp.exp2(score * (scale * LOG2E) - norm)
    if mask is not None:
        weight = jnp.where(mask, weight, 0.0)
    score_grad = (weight * (dweight - delta)).astype(BF16)
    value_part = jnp.dot(weight.astype(BF16), grows, preferred_element_type=F32)
    key_part = jnp.dot(score_grad, qrows, preferred_element_type=F32)
    query_part = lax.dot_general(keys, score_grad, TN, preferred_element_type=F32)
    return query_part, key_part, value_part


def block_rows(index, size):
    return pl.ds(pl.multiple_of(index * size, size), size)


def own_place(position, shard):
    return shard == position, 0


def near_place(position, shard):
    back = (position >> 1) - (shard >> 1)
    other = (position ^ shard) & 1
    return (back == 1) | ((back == 0) & (other == 1)), back + (back & other)


def far_place(position, shard):
    back = (position >> 1) - (shard >> 1)
    return back == 2, (position ^ shard) & 1


def listed_items(position, list_ref, live_ref, items_ref, place_of, shards):
    local_blocks, slots = list_ref.shape
    shift = local_blocks.bit_length() - 1
    doubles, singles = jnp.int32(0), jnp.int32(0)
    for step in range(local_blocks):

        def one(slot, carry, step=step):
            doubles, waiting, last = carry
            block = list_ref[step, slot]
            keep, place = place_of(position, block >> shift)
            keep = (keep & (block != position * local_blocks + step)).astype(jnp.int32)
            local = place * local_blocks + (block & (local_blocks - 1))
            code = step * CODES + local
            items_ref[0, doubles] = last * CODES * CODES + code
            doubles = doubles + (keep & waiting)
            return doubles, keep ^ waiting, jnp.where(keep == 1, code, last)

        doubles, waiting, last = lax.fori_loop(
            0, live_ref[step], one, (doubles, jnp.int32(0), jnp.int32(0))
        )
        items_ref[1, singles] = last
        singles = singles + waiting
    return doubles, singles


def run_items(counts, items_ref, k_ref, v_ref, q_ref, g_ref, norm_ref, delta_ref,
              dq_ref, dk_ref, dv_ref, scale):
    rows = norm_ref.shape[2]

    def some(row, start, number):
        entries = []
        for offset in range(number):
            item = items_ref[row, start + offset]
            places = [item & (CODES - 1)]
            if row == 0:
                places.append((item >> (2 * CODE_BITS)) & (CODES - 1))
            entries.append(((item >> CODE_BITS) & (CODES - 1), [block_rows(p, BLOCK) for p in places]))
        terms = []
        for step, spans in entries:
            span = block_rows(step, rows)
            keys = jnp.concatenate([k_ref[at, :] for at in spans], axis=0)
            values = jnp.concatenate([v_ref[at, :] for at in spans], axis=0)
            terms.append(
                tile_terms(
                    keys, values, q_ref[span, :], g_ref[span, :], norm_ref[step], delta_ref[step],
                    scale,
                )
            )
        for (step, spans), (dq, dk, dv) in zip(entries, terms):
            dq_ref[step] += dq
            for index, at in enumerate(spans):
                part = slice(index * BLOCK, (index + 1) * BLOCK)
                dk_ref[at, :] += dk[part]
                dv_ref[at, :] += dv[part]

    for row, count in enumerate(counts):

        def two(index, carry, row=row):
            some(row, index * 2, 2)
            return carry

        lax.fori_loop(0, count // 2, two, 0)

        @pl.when(count % 2 == 1)
        def _(row=row, count=count):
            some(row, count - 1, 1)


def own_kernel(
    position_ref, list_hbm, live_hbm, q_hbm, g_hbm, o_hbm, norm_hbm, both_ref,
    list_out, live_out, q_ref, g_ref, norm_ref, delta_ref, dq_ref, dk_ref, dv_ref,
    o_ref, raw_ref, list_ref, live_ref, items_ref, row_sems, sems, *, scale,
):
    local_blocks = list_ref.shape[0]
    head_size = q_ref.shape[1]
    rows = norm_ref.shape[2]
    heads = rows // BLOCK
    tokens = local_blocks * BLOCK
    k_ref, v_ref = both_ref.at[pl.ds(0, tokens), :], both_ref.at[pl.ds(tokens, tokens), :]
    single = [
        pltpu.make_async_copy(source, target, sems.at[index])
        for index, (source, target) in enumerate(
            (
                (norm_hbm, raw_ref), (list_hbm, list_ref),
                (live_hbm, live_ref), (list_hbm, list_out), (live_hbm, live_out),
            )
        )
    ]
    moves = []
    for step in range(local_blocks):
        span = pl.ds(step * rows, rows)
        moves.append([
            pltpu.make_async_copy(source.at[span, :], target.at[span, :], row_sems.at[index, step])
            for index, (source, target) in enumerate(
                ((g_hbm, g_ref), (o_hbm, o_ref), (q_hbm, q_ref))
            )
        ])
    for copy in moves[0] + single + moves[1] + moves[2] + moves[3]:
        copy.start()
    ones = jnp.ones((8, 2 * head_size), BF16)
    key_pos = lax.broadcasted_iota(jnp.int32, (BLOCK, rows), 0)
    row_pos = lax.broadcasted_iota(jnp.int32, (BLOCK, rows), 1)
    mask = key_pos * heads <= row_pos
    same_token = jnp.where(key_pos == row_pos // heads, 1.0, 0.0).astype(BF16)
    head_pos = lax.broadcasted_iota(jnp.int32, (3 * heads, rows), 0) % heads
    same_head = head_pos == lax.broadcasted_iota(jnp.int32, (3 * heads, rows), 1) % heads
    for copy in single:
        copy.wait()
    for step in range(local_blocks):
        span = pl.ds(step * rows, rows)
        at = pl.ds(step * BLOCK, BLOCK)
        rest = raw_ref[:, at] * LOG2E
        pieces = []
        for _ in range(3):
            pieces.append(rest.astype(BF16).astype(F32))
            rest = rest - pieces[-1]
        pieces = jnp.concatenate(pieces, axis=0).astype(BF16)
        spread = jnp.dot(pieces, same_token, preferred_element_type=F32)
        norm = jnp.sum(jnp.where(same_head, spread, 0.0), axis=0, keepdims=True)
        norm_ref[step] = norm
        for copy in moves[step]:
            copy.wait()
        product = g_ref[span, :].astype(F32) * o_ref[span, :].astype(F32)
        high = product.astype(BF16)
        low = (product - high.astype(F32)).astype(BF16)
        both = jnp.concatenate([high, low], axis=1)
        delta = lax.dot_general(ones, both, NT, preferred_element_type=F32)
        delta_ref[step] = delta[:1]
        dq, dk, dv = tile_terms(
            k_ref[at, :], v_ref[at, :], q_ref[span, :], g_ref[span, :], norm, delta[:1], scale, mask
        )
        dq_ref[step] = dq
        dk_ref[at, :] = dk
        dv_ref[at, :] = dv
    counts = listed_items(position_ref[0], list_ref, live_ref, items_ref, own_place, 1)
    run_items(
        counts, items_ref, k_ref, v_ref, q_ref, g_ref, norm_ref, delta_ref,
        dq_ref, dk_ref, dv_ref, scale,
    )
    dk_ref[...] = dk_ref[...] * scale


def shards_kernel(position_ref, list_ref, live_ref, q_ref, g_ref, norm_ref, delta_ref, *refs,
                  scale, parts, shards, place_of):
    tokens = list_ref.shape[0] * BLOCK
    inputs = []
    for ref in refs[1 : 1 + parts]:
        inputs += [ref.at[pl.ds(start, tokens), :] for start in range(0, ref.shape[0], tokens)]
    dq_ref = refs[1 + parts]
    outs = refs[2 + parts : -5]
    k_all, v_all, dk_acc, dv_acc, items_ref = refs[-5:]
    counts = listed_items(position_ref[0], list_ref, live_ref, items_ref, place_of, shards)
    for index in range(shards):
        span = pl.ds(index * tokens, tokens)
        k_all[span, :] = inputs[2 * index][...]
        v_all[span, :] = inputs[2 * index + 1][...]
    dk_acc[...] = jnp.zeros_like(dk_acc)
    dv_acc[...] = jnp.zeros_like(dv_acc)
    run_items(
        counts, items_ref, k_all, v_all, q_ref, g_ref, norm_ref,
        delta_ref, dq_ref, dk_acc, dv_acc, scale,
    )
    pieces = len(outs) - shards + 1
    size = 2 * tokens // pieces
    for index in range(pieces // 2):
        span = pl.ds((shards - 1) * tokens + index * size, size)
        outs[index][...] = (dk_acc[span, :] * scale).astype(BF16)
        outs[pieces // 2 + index][...] = dv_acc[span, :].astype(BF16)
    for ref, place in zip(outs[pieces:], range(shards - 2, -1, -1)):
        span = pl.ds(place * tokens, tokens)
        ref[pl.ds(0, tokens), :] = (dk_acc[span, :] * scale).astype(BF16)
        ref[pl.ds(tokens, tokens), :] = dv_acc[span, :].astype(BF16)


def add_kernel(straight_ref, *refs, outs):
    crossed, out_refs = refs[:-outs], refs[-outs:]
    size = crossed[0].shape[0]
    whole = len(crossed) * size // outs
    for index, ref in enumerate(crossed):
        span = pl.ds(index * size, size)
        out_span = pl.ds(index * size % whole, size)
        total = straight_ref[span, :].astype(F32) + ref[...].astype(F32)
        out_refs[index * size // whole][out_span, :] = total.astype(BF16)
    if outs == 1:
        span = pl.ds(whole, SPARE)
        out_refs[0][span, :] = jnp.zeros((SPARE, straight_ref.shape[1]), BF16)


def stack_kernel(k_hbm, v_hbm, out_ref, sems):
    tokens = k_hbm.shape[0]
    copies = [
        pltpu.make_async_copy(source, out_ref.at[pl.ds(half * tokens, tokens), :], sems.at[half])
        for half, source in enumerate((k_hbm, v_hbm))
    ]
    for copy in copies:
        copy.start()
    for copy in copies:
        copy.wait()


def finish_kernel(dq_ref, out_ref, *, scale):
    out_ref[...] = (dq_ref[0] * scale).T.astype(out_ref.dtype)


def in_vmem(array):
    return pltpu.with_memory_space_constraint(array, pltpu.VMEM)


def in_hbm(array):
    return pltpu.with_memory_space_constraint(array, pltpu.HBM)


def body(
    queries, key_tokens, value_tokens, out_grad, forward_out, log_norm, block_list, block_live
):
    local_tokens, heads, head_size = queries.shape
    local_blocks, slots = block_list.shape
    rows = BLOCK * heads
    all_rows = (local_blocks * rows, head_size)
    scale = head_size ** (-0.5)
    position = lax.axis_index(AXES).astype(jnp.int32)
    device = position.reshape(1)

    smem = pl.BlockSpec(memory_space=pltpu.SMEM)
    vmem = pl.BlockSpec(memory_space=pltpu.VMEM)
    anywhere = pl.BlockSpec(memory_space=pl.ANY)
    line_shape = pltpu.VMEM((local_blocks, 1, rows), F32)
    rows_shape = pltpu.VMEM(all_rows, BF16)
    dq_shape = pltpu.VMEM((local_blocks, head_size, rows), F32)
    wide_shape = jax.ShapeDtypeStruct((local_tokens, head_size), F32)
    spare_shape = jax.ShapeDtypeStruct((2 * local_tokens + SPARE, head_size), BF16)
    quarter = jax.ShapeDtypeStruct((local_tokens // 2, head_size), BF16)
    items = pltpu.SMEM((2, local_blocks * slots + 1), jnp.int32)
    params = pltpu.CompilerParams(vmem_limit_bytes=24 * 1024 * 1024)

    def stacked(number):
        return jax.ShapeDtypeStruct((number * local_tokens, head_size), BF16)

    def cost(slots):
        return pl.CostEstimate(flops=slots, bytes_accessed=slots, transcendentals=0)

    def own_call():
        outs = pl.pallas_call(
            functools.partial(own_kernel, scale=scale),
            in_specs=[smem] + [anywhere] * 6 + [vmem],
            out_specs=[vmem] * 9,
            out_shape=[pltpu.VMEM(block_list.shape, jnp.int32)]
            + [pltpu.VMEM(block_live.shape, jnp.int32)]
            + [rows_shape] * 2 + [line_shape] * 2 + [dq_shape] + [wide_shape] * 2,
            scratch_shapes=[
                pltpu.VMEM(all_rows, BF16), pltpu.VMEM((heads, local_tokens), F32),
                pltpu.SMEM(block_list.shape, jnp.int32), pltpu.SMEM(block_live.shape, jnp.int32),
                items, pltpu.SemaphoreType.DMA((3, local_blocks)), pltpu.SemaphoreType.DMA((5,)),
            ],
            compiler_params=params,
            cost_estimate=cost(1),
            name="own_shard",
        )(
            device, in_hbm(block_list), in_hbm(block_live),
            in_hbm(queries.reshape(all_rows)), in_hbm(out_grad.reshape(all_rows)),
            in_hbm(forward_out.reshape(all_rows)), in_hbm(log_norm.T),
            in_vmem(kv),
        )
        return [in_vmem(x) for x in outs[:7]] + list(outs[7:])

    def shards_call(dq, parts, shards, place_of, name):
        wide = pltpu.VMEM((shards * local_tokens, head_size), F32)
        narrow = pltpu.VMEM((shards * local_tokens, head_size), BF16)
        return pl.pallas_call(
            functools.partial(
                shards_kernel, scale=scale, parts=len(parts), shards=shards, place_of=place_of
            ),
            in_specs=[smem] * 3 + [vmem] * (5 + len(parts)),
            out_specs=[vmem] * (shards + 2),
            out_shape=[dq_shape]
            + [stacked(1)] * 2
            + [stacked(2)] * (shards - 1),
            scratch_shapes=[narrow, narrow, wide, wide, items],
            input_output_aliases={7: 0},
            compiler_params=params,
            cost_estimate=cost(1),
            name=name,
        )(device, listed, live, q, g, norm, delta, in_vmem(dq), *map(in_vmem, parts))

    def add_call(straight, crossed, shapes, name):
        return pl.pallas_call(
            functools.partial(add_kernel, outs=len(shapes)),
            in_specs=[vmem] * (1 + len(crossed)),
            out_specs=[vmem] * len(shapes),
            out_shape=shapes,
            compiler_params=params,
            cost_estimate=cost(1),
            name=name,
        )(*map(in_vmem, (straight, *crossed)))

    def stack_call():
        return pl.pallas_call(
            stack_kernel,
            in_specs=[anywhere] * 2,
            out_specs=vmem,
            out_shape=stacked(2),
            scratch_shapes=[pltpu.SemaphoreType.DMA((2,))],
            compiler_params=params,
            cost_estimate=cost(1),
            name="stack",
        )(in_hbm(key_tokens), in_hbm(value_tokens))

    def finish_call(dq):
        return pl.pallas_call(
            functools.partial(finish_kernel, scale=scale),
            grid=(local_blocks,),
            in_specs=[pl.BlockSpec((1, head_size, rows), lambda i: (i, 0, 0))],
            out_specs=pl.BlockSpec((rows, head_size), lambda i: (i, 0)),
            out_shape=jax.ShapeDtypeStruct(all_rows, BF16),
            compiler_params=params,
            cost_estimate=cost(1),
            name="query_grad",
        )(in_vmem(dq))

    k2, v2 = ring_shift(key_tokens, 2), ring_shift(value_tokens, 2)
    kv = stack_call()
    kv4 = ring_shift(kv, 4)
    listed, live, q, g, norm, delta, dq, dk0, dv0 = own_call()
    k2, v2, dq = lax.optimization_barrier((k2, v2, dq))
    dq, *crossed, near, other = shards_call(
        dq, (pair_swap(kv), k2, v2, pair_swap(k2), pair_swap(v2)), 3, near_place, "near_shards"
    )
    (near,) = add_call(near, [pair_swap(x) for x in crossed], [spare_shape], "near_sum")
    near = ring_shift(near, -2)
    kv4, dq = lax.optimization_barrier((kv4, dq))
    dq, *crossed, far = shards_call(dq, (kv4, pair_swap(kv4)), 2, far_place, "far_shards")
    far = add_call(far, [pair_swap(x) for x in crossed], [stacked(1)] * 2, "far_sum")
    far_k, far_v = (ring_shift(part, -4) for part in far)
    near, dq = lax.optimization_barrier((near, dq))
    query_grad = finish_call(dq)
    far_k, far_v, query_grad = lax.optimization_barrier((far_k, far_v, query_grad))
    rest = pair_swap(other).astype(F32) + near[: 2 * local_tokens].astype(F32)
    key_grad = (dk0 + rest[:local_tokens] + far_k.astype(F32)).astype(BF16)
    value_grad = (dv0 + rest[local_tokens:] + far_v.astype(F32)).astype(BF16)
    return query_grad.reshape(queries.shape), key_grad, value_grad


def solution(mesh):
    tokens = P(AXES, None)
    wide = P(AXES, None, None)
    return jax.shard_map(
        body,
        mesh=mesh,
        in_specs=(wide, tokens, tokens, wide, wide, tokens, tokens, P(AXES)),
        out_specs=(wide, tokens, tokens),
        check_vma=False,
    )
```

```python
import functools

import jax
import jax.numpy as jnp
from jax import lax
from jax.experimental import pallas as pl
from jax.experimental.pallas import tpu as pltpu
from jax.sharding import PartitionSpec as P

BLOCK = 128
CODE_BITS = 4
CODES = 1 << CODE_BITS
SPARE = 16
AXES = ("inner", "outer")
LOG2E = 1.4426950408889634
NT = (((1,), (1,)), ((), ()))
TN = (((0,), (0,)), ((), ()))
F32 = jnp.float32
BF16 = jnp.bfloat16


def ring_shift(block, distance):
    count = lax.axis_size(AXES)
    route = [(i, (i + distance) % count) for i in range(count)]
    return lax.ppermute(block, AXES, route)


def pair_swap(block):
    count = lax.axis_size(AXES)
    return lax.ppermute(block, AXES, [(i, i ^ 1) for i in range(count)])


def tile_terms(keys, values, qrows, grows, norm, delta, scale, mask=None):
    score = lax.dot_general(keys, qrows, NT, preferred_element_type=F32)
    dweight = lax.dot_general(values, grows, NT, preferred_element_type=F32)
    weight = jnp.exp2(score * (scale * LOG2E) - norm)
    if mask is not None:
        weight = jnp.where(mask, weight, 0.0)
    score_grad = (weight * (dweight - delta)).astype(BF16)
    value_part = jnp.dot(weight.astype(BF16), grows, preferred_element_type=F32)
    key_part = jnp.dot(score_grad, qrows, preferred_element_type=F32)
    query_part = lax.dot_general(keys, score_grad, TN, preferred_element_type=F32)
    return query_part, key_part, value_part


def block_rows(index, size):
    return pl.ds(pl.multiple_of(index * size, size), size)


def own_place(position, shard):
    return shard == position, 0


def near_place(position, shard):
    back = (position >> 1) - (shard >> 1)
    other = (position ^ shard) & 1
    return (back == 1) | ((back == 0) & (other == 1)), back + (back & other)


def far_place(position, shard):
    back = (position >> 1) - (shard >> 1)
    return back == 2, (position ^ shard) & 1


def listed_items(position, list_ref, live_ref, items_ref, place_of, shards):
    local_blocks, slots = list_ref.shape
    shift = local_blocks.bit_length() - 1
    doubles, singles = jnp.int32(0), jnp.int32(0)
    for step in range(local_blocks):

        def one(slot, carry, step=step):
            doubles, waiting, last = carry
            block = list_ref[step, slot]
            keep, place = place_of(position, block >> shift)
            keep = (keep & (block != position * local_blocks + step)).astype(jnp.int32)
            local = place * local_blocks + (block & (local_blocks - 1))
            code = step * CODES + local
            items_ref[0, doubles] = last * CODES * CODES + code
            doubles = doubles + (keep & waiting)
            return doubles, keep ^ waiting, jnp.where(keep == 1, code, last)

        doubles, waiting, last = lax.fori_loop(
            0, live_ref[step], one, (doubles, jnp.int32(0), jnp.int32(0))
        )
        items_ref[1, singles] = last
        singles = singles + waiting
    return doubles, singles


def run_items(counts, items_ref, k_ref, v_ref, q_ref, g_ref, norm_ref, delta_ref,
              dq_ref, dk_ref, dv_ref, scale):
    rows = norm_ref.shape[2]

    def some(row, start, number):
        entries = []
        for offset in range(number):
            item = items_ref[row, start + offset]
            places = [item & (CODES - 1)]
            if row == 0:
                places.append((item >> (2 * CODE_BITS)) & (CODES - 1))
            entries.append(((item >> CODE_BITS) & (CODES - 1), [block_rows(p, BLOCK) for p in places]))
        terms = []
        for step, spans in entries:
            span = block_rows(step, rows)
            keys = jnp.concatenate([k_ref[at, :] for at in spans], axis=0)
            values = jnp.concatenate([v_ref[at, :] for at in spans], axis=0)
            terms.append(
                tile_terms(
                    keys, values, q_ref[span, :], g_ref[span, :], norm_ref[step], delta_ref[step],
                    scale,
                )
            )
        for (step, spans), (dq, dk, dv) in zip(entries, terms):
            dq_ref[step] += dq
            for index, at in enumerate(spans):
                part = slice(index * BLOCK, (index + 1) * BLOCK)
                dk_ref[at, :] += dk[part]
                dv_ref[at, :] += dv[part]

    for row, count in enumerate(counts):

        def two(index, carry, row=row):
            some(row, index * 2, 2)
            return carry

        lax.fori_loop(0, count // 2, two, 0)

        @pl.when(count % 2 == 1)
        def _(row=row, count=count):
            some(row, count - 1, 1)


def own_kernel(
    position_ref, list_hbm, live_hbm, q_hbm, g_hbm, o_hbm, norm_hbm, both_ref,
    list_out, live_out, q_ref, g_ref, norm_ref, delta_ref, dq_ref, dk_ref, dv_ref,
    o_ref, raw_ref, list_ref, live_ref, items_ref, row_sems, sems, *, scale,
):
    local_blocks = list_ref.shape[0]
    head_size = q_ref.shape[1]
    rows = norm_ref.shape[2]
    heads = rows // BLOCK
    tokens = local_blocks * BLOCK
    k_ref, v_ref = both_ref.at[pl.ds(0, tokens), :], both_ref.at[pl.ds(tokens, tokens), :]
    single = [
        pltpu.make_async_copy(source, target, sems.at[index])
        for index, (source, target) in enumerate(
            (
                (norm_hbm, raw_ref), (list_hbm, list_ref),
                (live_hbm, live_ref), (list_hbm, list_out), (live_hbm, live_out),
            )
        )
    ]
    moves = []
    for step in range(local_blocks):
        span = pl.ds(step * rows, rows)
        moves.append([
            pltpu.make_async_copy(source.at[span, :], target.at[span, :], row_sems.at[index, step])
            for index, (source, target) in enumerate(
                ((g_hbm, g_ref), (o_hbm, o_ref), (q_hbm, q_ref))
            )
        ])
    for copy in moves[0] + single + moves[1] + moves[2] + moves[3]:
        copy.start()
    ones = jnp.ones((8, 2 * head_size), BF16)
    key_pos = lax.broadcasted_iota(jnp.int32, (BLOCK, rows), 0)
    row_pos = lax.broadcasted_iota(jnp.int32, (BLOCK, rows), 1)
    mask = key_pos * heads <= row_pos
    same_token = jnp.where(key_pos == row_pos // heads, 1.0, 0.0).astype(BF16)
    head_pos = lax.broadcasted_iota(jnp.int32, (3 * heads, rows), 0) % heads
    same_head = head_pos == lax.broadcasted_iota(jnp.int32, (3 * heads, rows), 1) % heads
    for copy in single:
        copy.wait()
    for step in range(local_blocks):
        span = pl.ds(step * rows, rows)
        at = pl.ds(step * BLOCK, BLOCK)
        rest = raw_ref[:, at] * LOG2E
        pieces = []
        for _ in range(3):
            pieces.append(rest.astype(BF16).astype(F32))
            rest = rest - pieces[-1]
        pieces = jnp.concatenate(pieces, axis=0).astype(BF16)
        spread = jnp.dot(pieces, same_token, preferred_element_type=F32)
        norm = jnp.sum(jnp.where(same_head, spread, 0.0), axis=0, keepdims=True)
        norm_ref[step] = norm
        for copy in moves[step]:
            copy.wait()
        product = g_ref[span, :].astype(F32) * o_ref[span, :].astype(F32)
        high = product.astype(BF16)
        low = (product - high.astype(F32)).astype(BF16)
        both = jnp.concatenate([high, low], axis=1)
        delta = lax.dot_general(ones, both, NT, preferred_element_type=F32)
        delta_ref[step] = delta[:1]
        dq, dk, dv = tile_terms(
            k_ref[at, :], v_ref[at, :], q_ref[span, :], g_ref[span, :], norm, delta[:1], scale, mask
        )
        dq_ref[step] = dq
        dk_ref[at, :] = dk
        dv_ref[at, :] = dv
    counts = listed_items(position_ref[0], list_ref, live_ref, items_ref, own_place, 1)
    run_items(
        counts, items_ref, k_ref, v_ref, q_ref, g_ref, norm_ref, delta_ref,
        dq_ref, dk_ref, dv_ref, scale,
    )
    dk_ref[...] = dk_ref[...] * scale


def shards_kernel(position_ref, list_ref, live_ref, q_ref, g_ref, norm_ref, delta_ref, *refs,
                  scale, parts, shards, place_of):
    tokens = list_ref.shape[0] * BLOCK
    inputs = []
    for ref in refs[1 : 1 + parts]:
        inputs += [ref.at[pl.ds(start, tokens), :] for start in range(0, ref.shape[0], tokens)]
    dq_ref = refs[1 + parts]
    outs = refs[2 + parts : -5]
    k_all, v_all, dk_acc, dv_acc, items_ref = refs[-5:]
    counts = listed_items(position_ref[0], list_ref, live_ref, items_ref, place_of, shards)
    for index in range(shards):
        span = pl.ds(index * tokens, tokens)
        k_all[span, :] = inputs[2 * index][...]
        v_all[span, :] = inputs[2 * index + 1][...]
    dk_acc[...] = jnp.zeros_like(dk_acc)
    dv_acc[...] = jnp.zeros_like(dv_acc)
    run_items(
        counts, items_ref, k_all, v_all, q_ref, g_ref, norm_ref,
        delta_ref, dq_ref, dk_acc, dv_acc, scale,
    )
    pieces = 2
    size = 2 * tokens // pieces
    for index in range(pieces // 2):
        span = pl.ds((shards - 1) * tokens + index * size, size)
        outs[index][...] = (dk_acc[span, :] * scale).astype(BF16)
        outs[pieces // 2 + index][...] = dv_acc[span, :].astype(BF16)
    if shards == 2:
        outs[2][...] = (dk_acc[pl.ds(0, tokens), :] * scale).astype(BF16)
        outs[3][...] = dv_acc[pl.ds(0, tokens), :].astype(BF16)
        return
    for ref, place in zip(outs[pieces:], range(shards - 2, -1, -1)):
        span = pl.ds(place * tokens, tokens)
        ref[pl.ds(0, tokens), :] = (dk_acc[span, :] * scale).astype(BF16)
        ref[pl.ds(tokens, tokens), :] = dv_acc[span, :].astype(BF16)


def add_kernel(straight_ref, *refs, outs):
    crossed, out_refs = refs[:-outs], refs[-outs:]
    size = crossed[0].shape[0]
    whole = len(crossed) * size // outs
    for index, ref in enumerate(crossed):
        span = pl.ds(index * size, size)
        out_span = pl.ds(index * size % whole, size)
        total = straight_ref[span, :].astype(F32) + ref[...].astype(F32)
        out_refs[index * size // whole][out_span, :] = total.astype(BF16)
    if out_refs[0].shape[0] > whole:
        span = pl.ds(whole, SPARE)
        out_refs[0][span, :] = jnp.zeros((SPARE, straight_ref.shape[1]), BF16)


def stack_kernel(k_hbm, v_hbm, out_ref, sems):
    tokens = k_hbm.shape[0]
    copies = [
        pltpu.make_async_copy(source, out_ref.at[pl.ds(half * tokens, tokens), :], sems.at[half])
        for half, source in enumerate((k_hbm, v_hbm))
    ]
    for copy in copies:
        copy.start()
    for copy in copies:
        copy.wait()


def finish_kernel(dq_ref, out_ref, *, scale):
    out_ref[...] = (dq_ref[0] * scale).T.astype(out_ref.dtype)


def in_vmem(array):
    return pltpu.with_memory_space_constraint(array, pltpu.VMEM)


def in_hbm(array):
    return pltpu.with_memory_space_constraint(array, pltpu.HBM)


def body(
    queries, key_tokens, value_tokens, out_grad, forward_out, log_norm, block_list, block_live
):
    local_tokens, heads, head_size = queries.shape
    local_blocks, slots = block_list.shape
    rows = BLOCK * heads
    all_rows = (local_blocks * rows, head_size)
    scale = head_size ** (-0.5)
    position = lax.axis_index(AXES).astype(jnp.int32)
    device = position.reshape(1)

    smem = pl.BlockSpec(memory_space=pltpu.SMEM)
    vmem = pl.BlockSpec(memory_space=pltpu.VMEM)
    anywhere = pl.BlockSpec(memory_space=pl.ANY)
    line_shape = pltpu.VMEM((local_blocks, 1, rows), F32)
    rows_shape = pltpu.VMEM(all_rows, BF16)
    dq_shape = pltpu.VMEM((local_blocks, head_size, rows), F32)
    wide_shape = jax.ShapeDtypeStruct((local_tokens, head_size), F32)
    spare_shape = jax.ShapeDtypeStruct((2 * local_tokens + SPARE, head_size), BF16)
    quarter = jax.ShapeDtypeStruct((local_tokens // 2, head_size), BF16)
    items = pltpu.SMEM((2, local_blocks * slots + 1), jnp.int32)
    params = pltpu.CompilerParams(vmem_limit_bytes=24 * 1024 * 1024)

    def stacked(number):
        return jax.ShapeDtypeStruct((number * local_tokens, head_size), BF16)

    def cost(slots):
        return pl.CostEstimate(flops=slots, bytes_accessed=slots, transcendentals=0)

    def own_call():
        outs = pl.pallas_call(
            functools.partial(own_kernel, scale=scale),
            in_specs=[smem] + [anywhere] * 6 + [vmem],
            out_specs=[vmem] * 9,
            out_shape=[pltpu.VMEM(block_list.shape, jnp.int32)]
            + [pltpu.VMEM(block_live.shape, jnp.int32)]
            + [rows_shape] * 2 + [line_shape] * 2 + [dq_shape] + [wide_shape] * 2,
            scratch_shapes=[
                pltpu.VMEM(all_rows, BF16), pltpu.VMEM((heads, local_tokens), F32),
                pltpu.SMEM(block_list.shape, jnp.int32), pltpu.SMEM(block_live.shape, jnp.int32),
                items, pltpu.SemaphoreType.DMA((3, local_blocks)), pltpu.SemaphoreType.DMA((5,)),
            ],
            compiler_params=params,
            cost_estimate=cost(1),
            name="own_shard",
        )(
            device, in_hbm(block_list), in_hbm(block_live),
            in_hbm(queries.reshape(all_rows)), in_hbm(out_grad.reshape(all_rows)),
            in_hbm(forward_out.reshape(all_rows)), in_hbm(log_norm.T),
            in_vmem(kv),
        )
        return [in_vmem(x) for x in outs[:7]] + list(outs[7:])

    def shards_call(dq, parts, shards, place_of, name):
        wide = pltpu.VMEM((shards * local_tokens, head_size), F32)
        narrow = pltpu.VMEM((shards * local_tokens, head_size), BF16)
        return pl.pallas_call(
            functools.partial(
                shards_kernel, scale=scale, parts=len(parts), shards=shards, place_of=place_of
            ),
            in_specs=[smem] * 3 + [vmem] * (5 + len(parts)),
            out_specs=[vmem] * 5,
            out_shape=[dq_shape]
            + [stacked(1)] * 2
            + [stacked(shards - 1)] * 2,
            scratch_shapes=[narrow, narrow, wide, wide, items],
            input_output_aliases={7: 0},
            compiler_params=params,
            cost_estimate=cost(1),
            name=name,
        )(device, listed, live, q, g, norm, delta, in_vmem(dq), *map(in_vmem, parts))

    def add_call(straight, crossed, shapes, name):
        return pl.pallas_call(
            functools.partial(add_kernel, outs=len(shapes)),
            in_specs=[vmem] * (1 + len(crossed)),
            out_specs=[vmem] * len(shapes),
            out_shape=shapes,
            compiler_params=params,
            cost_estimate=cost(1),
            name=name,
        )(*map(in_vmem, (straight, *crossed)))

    def stack_call():
        return pl.pallas_call(
            stack_kernel,
            in_specs=[anywhere] * 2,
            out_specs=vmem,
            out_shape=stacked(2),
            scratch_shapes=[pltpu.SemaphoreType.DMA((2,))],
            compiler_params=params,
            cost_estimate=cost(1),
            name="stack",
        )(in_hbm(key_tokens), in_hbm(value_tokens))

    def finish_call(dq):
        return pl.pallas_call(
            functools.partial(finish_kernel, scale=scale),
            grid=(local_blocks,),
            in_specs=[pl.BlockSpec((1, head_size, rows), lambda i: (i, 0, 0))],
            out_specs=pl.BlockSpec((rows, head_size), lambda i: (i, 0)),
            out_shape=jax.ShapeDtypeStruct(all_rows, BF16),
            compiler_params=params,
            cost_estimate=cost(1),
            name="query_grad",
        )(in_vmem(dq))

    k2, v2 = ring_shift(key_tokens, 2), ring_shift(value_tokens, 2)
    kv = stack_call()
    kv4 = ring_shift(kv, 4)
    listed, live, q, g, norm, delta, dq, dk0, dv0 = own_call()
    k2, v2, dq = lax.optimization_barrier((k2, v2, dq))
    dq, *crossed, near, other = shards_call(
        dq,
        (pair_swap(kv), k2, v2, pair_swap(k2), pair_swap(v2)),
        3, near_place, "near_shards",
    )
    (near,) = add_call(near, [pair_swap(x) for x in crossed], [spare_shape], "near_sum")
    near = ring_shift(near, -2)
    kv4, dq = lax.optimization_barrier((kv4, dq))
    dq, *parts = shards_call(dq, (kv4, pair_swap(kv4)), 2, far_place, "far_shards")
    crossed, far = parts[:2], parts[2:]
    far_k, far_v = (
        ring_shift(add_call(part, [pair_swap(x)], [stacked(1)], "far_sum")[0], -4)
        for part, x in zip(far, crossed)
    )
    near, dq = lax.optimization_barrier((near, dq))
    query_grad = finish_call(dq)
    far_k, far_v, query_grad = lax.optimization_barrier((far_k, far_v, query_grad))
    rest = pair_swap(other).astype(F32) + near[: 2 * local_tokens].astype(F32)
    key_grad = (dk0 + rest[:local_tokens] + far_k.astype(F32)).astype(BF16)
    value_grad = (dv0 + rest[local_tokens:] + far_v.astype(F32)).astype(BF16)
    return query_grad.reshape(queries.shape), key_grad, value_grad


def solution(mesh):
    tokens = P(AXES, None)
    wide = P(AXES, None, None)
    return jax.shard_map(
        body,
        mesh=mesh,
        in_specs=(wide, tokens, tokens, wide, wide, tokens, tokens, P(AXES)),
        out_specs=(wide, tokens, tokens),
        check_vma=False,
    )
```
